512 devices in a mesh: seq: 64 (over z, y_lo, core), tp: 8 (over y_hi, x).
Axes of the slice: x: 4, y: 4 (y_hi: 2, y_lo: 2; y = y_hi * 2 + y_lo), z: 16, core: 2. Of those that a mesh axis runs over, the one named last changes fastest.
Arguments:
- queries: bfloat16 [8192, 1024], P('seq'), may hold values from -8 to 8
- key_rows: bfloat16 [8192, 256], P(('seq', 'tp')), may hold values from -4 to 4
- value_rows: bfloat16 [8192, 256], P(('seq', 'tp')), may hold values from -6 to 6
- ssm_input: bfloat16 [8192, 3072], P('seq', 'tp'), may hold values from -0.29882812 to 0.29882812
- gate_input: bfloat16 [8192, 3072], P('seq', 'tp'), may hold values from -6 to 6
- write_vectors: bfloat16 [8192, 256], P('seq'), may hold values from -1.5 to 1.5
- read_vectors: bfloat16 [8192, 256], P('seq'), may hold values from -1.5 to 1.5
- decay_rates: float32 [8192, 48], P('seq', 'tp'), may hold values from 0 to 3, as said below
- attn_out_weight: bfloat16 [1024, 2048], P('tp'), may hold values from -0.8984375 to 0.8984375
- ssm_out_weight: bfloat16 [3072, 2048], P('tp'), may hold values from -0.109375 to 0.109375
Outputs:
- mixer_output: float32 [8192, 2048], P(('seq', 'tp'))
The draws below stay inside these ranges and needn't reach their ends.
Inputs may be any that keep to these rules, and one draw needn't show every extreme that they name: `decay_rates`: positive.
All inputs are finite; a program needn't handle non-finite values.
Results may differ from the reference program's by a relative error of at most 0.0045.
Values may be sent and summed in bfloat16 or wider, within the bound.
No kernel may reach another device: no remote copies, remote signals or barrier semaphores. Data moves between devices by JAX's collectives and lax.ppermute only.
A program may use at most 128 MiB of HBM per device.

```python
import math
import jax
import jax.numpy as jnp
from jax import lax

D = 2048
HEADS = 48
HDIM = 64
STATE = 256
ASKER_PROBES = 8
KVHEADS = 2
HEAD = 128
TOK_DEV = 128
TOKENS = 8192


def shared_signs(key):
    picked = jax.random.uniform(jax.random.fold_in(key, 4401), (KVHEADS, HEAD))
    return jnp.where(picked < 0.5, -1.0, 1.0).astype(jnp.float32)


def draw_queries(key, part):
    inner_key = jax.random.fold_in(key, 17)
    shape = (TOKENS, ASKER_PROBES * HEAD)
    bulk = 2.5 * jax.random.truncated_normal(inner_key, -3.2, 3.2, shape, jnp.float32)
    pattern = jnp.repeat(shared_signs(key), ASKER_PROBES // KVHEADS, axis=0).reshape(-1)
    location_indices = jnp.array([TOKENS // 4 + 3, TOKENS // 2 + 5, 3 * TOKENS // 4 + 7, TOKENS - 1], jnp.int32)
    levels = jnp.array([4.5, 6.0, 7.0, 8.0], jnp.float32)
    similarity_logits = jnp.arange(TOKENS, dtype=jnp.int32)[:, None] == location_indices[None, :]
    strength = jnp.max(jnp.where(similarity_logits, levels[None, :], 0.0), axis=1)
    chosen = jnp.any(similarity_logits, axis=1)
    bulk = jnp.where(chosen[:, None], strength[:, None] * pattern[None, :], bulk)
    return bulk.astype(jnp.bfloat16)


def draw_key_rows(key, part):
    inner_key = jax.random.fold_in(key, 23)
    shape = (TOKENS, KVHEADS * HEAD)
    bulk = jax.random.truncated_normal(inner_key, -4.0, 4.0, shape, jnp.float32)
    pattern = shared_signs(key).reshape(-1)
    row_ids = jnp.arange(TOKENS, dtype=jnp.int32)[:, None]
    bulk = jnp.where(row_ids == 1, 4.0 * pattern[None, :], bulk)
    bulk = jnp.where(row_ids == 2, 3.96875 * pattern[None, :], bulk)
    return bulk.astype(jnp.bfloat16)


def draw_decay_rates(key, part):
    portion_lookup_vectors = jax.random.split(jax.random.fold_in(key, 31), 7)
    fast_share = 0.5
    fast = jax.random.uniform(portion_lookup_vectors[0], (HEADS,)) < fast_share
    fast_rate = jnp.exp(jax.random.uniform(portion_lookup_vectors[1], (HEADS,), jnp.float32, jnp.log(1.0 / 50.0), jnp.log(1.0 / 25.0)))
    slower_decay_rate = 0.3 * jnp.log(10.0) / TOKENS * jnp.exp(jax.random.uniform(portion_lookup_vectors[2], (HEADS,), jnp.float32, -0.69, 0.69))
    head_rate = jnp.where(fast, fast_rate, slower_decay_rate)
    block_factor = jnp.exp(jax.random.uniform(portion_lookup_vectors[3], (TOKENS // TOK_DEV, HEADS), jnp.float32, -0.69, 0.69))
    spread = jnp.repeat(block_factor, TOK_DEV, axis=0)
    rough = jax.random.uniform(portion_lookup_vectors[4], (TOKENS, HEADS), jnp.float32, 0.5, 1.5)
    location_indices = jax.random.randint(portion_lookup_vectors[5], (3,), 0, TOKENS)
    prompt_portions = jax.random.uniform(portion_lookup_vectors[6], (3,), jnp.float32, 0.22, 0.69)
    similarity_logits = jnp.arange(TOKENS, dtype=jnp.int32)[:, None] == location_indices[None, :]
    recurrence_transitions = jnp.sum(jnp.where(similarity_logits, prompt_portions[None, :], 0.0), axis=1)
    return head_rate[None, :] * spread * rough + recurrence_transitions[:, None]


def shard_levels(key, shape, cuts, least, largest):
    loudness, own = 1.0, jax.random.fold_in(key, 6)
    for dim, parts in cuts:
        draws = jnp.exp(jax.random.uniform(jax.random.fold_in(own, dim), (parts,), jnp.float32, least / len(cuts), largest / len(cuts)))
        loudness = loudness * jnp.repeat(draws, shape[dim] // parts).reshape([-1 if axis == dim else 1 for axis in range(len(shape))])
    return loudness


def bell_draw(own_key, shape, scale, most, cuts=(), kind=jnp.bfloat16):
    entries = jax.random.normal(own_key, shape, jnp.float32) * scale
    if len(cuts) > 0:
        entries = shard_levels(own_key, shape, cuts, -0.22, 0.18) * entries
    return jnp.clip(entries, min=-most, max=most).astype(kind)


def setup_inputs(seed: int = 0) -> dict:
    key_list = jax.random.split(jax.random.key(seed), 11)
    queries = draw_queries(jax.random.fold_in(key_list[10], 71), 0)
    key_rows = draw_key_rows(jax.random.fold_in(key_list[10], 71), 0)
    value_rows = bell_draw(key_list[2], (TOKENS, KVHEADS * HEAD), 1.0, 6.0, ((0, 512),))
    ssm_input = bell_draw(key_list[3], (TOKENS, HEADS * HDIM), 0.05, 0.29882812, ((0, 64), (1, 8)))
    gate_input = bell_draw(key_list[4], (TOKENS, HEADS * HDIM), 1.0, 6.0, ((0, 64), (1, 8)))
    write_vectors = bell_draw(key_list[5], (TOKENS, STATE), 0.25, 1.5, ((0, 64),))
    read_vectors = bell_draw(key_list[6], (TOKENS, STATE), 0.25, 1.5, ((0, 64),))
    decay_rates = draw_decay_rates(jax.random.fold_in(key_list[10], 71), 0)
    attn_out_weight = bell_draw(key_list[8], (ASKER_PROBES * HEAD, D), 0.15, 0.8984375, ((0, 8),))
    ssm_out_weight = bell_draw(key_list[9], (HEADS * HDIM, D), (HEADS * HDIM) ** -0.5, 0.109375, ((0, 8),))
    return {"queries": queries, "key_rows": key_rows, "value_rows": value_rows, "ssm_input": ssm_input, "gate_input": gate_input, "write_vectors": write_vectors, "read_vectors": read_vectors, "decay_rates": decay_rates, "attn_out_weight": attn_out_weight, "ssm_out_weight": ssm_out_weight}


precise = lax.Precision.HIGHEST

def ssm_block(carried_state, pieces):
    values_f32, write_f32, read_f32, rates = pieces
    block_rows = values_f32.shape[0]
    decay_sum = jnp.cumsum(-rates, axis=0)
    block_decay = decay_sum[-1]
    positions = jnp.arange(block_rows)
    causal = (positions[:, None] >= positions[None, :])[:, :, None]
    decay_gap = jnp.where(causal, decay_sum[:, None, :] - decay_sum[None, :, :], 0.0)
    decays = jnp.where(causal, jnp.exp(decay_gap), 0.0)
    read_write = jnp.dot(read_f32, write_f32.T, precision=precise)
    within = jnp.einsum('tsh,ts,shp->thp', decays, read_write, values_f32, precision=precise)
    from_before = jnp.einsum('th,tn,hpn->thp', jnp.exp(decay_sum), read_f32, carried_state, precision=precise)
    block_state = jnp.einsum('sh,shp,sn->hpn', jnp.exp(block_decay[None, :] - decay_sum), values_f32, write_f32, precision=precise)
    next_state = jnp.exp(block_decay)[:, None, None] * carried_state + block_state
    return (next_state, within + from_before)

def reference(queries, key_rows, value_rows, ssm_input, gate_input, write_vectors, read_vectors, decay_rates, attn_out_weight, ssm_out_weight):
    blocks = TOKENS // TOK_DEV
    values_f32 = ssm_input.astype(jnp.float32).reshape(blocks, TOK_DEV, HEADS, HDIM)
    write_f32 = write_vectors.astype(jnp.float32).reshape(blocks, TOK_DEV, STATE)
    read_f32 = read_vectors.astype(jnp.float32).reshape(blocks, TOK_DEV, STATE)
    rates = decay_rates.reshape(blocks, TOK_DEV, HEADS)
    initial = jnp.zeros((HEADS, HDIM, STATE), jnp.float32)
    _, ssm_raw = lax.scan(ssm_block, initial, (values_f32, write_f32, read_f32, rates))
    ssm_raw = ssm_raw.reshape(TOKENS, HEADS * HDIM)
    ssm_out = (ssm_raw * jax.nn.silu(gate_input.astype(jnp.float32))).astype(jnp.bfloat16)
    group = ASKER_PROBES // KVHEADS
    query_all = queries.astype(jnp.float32).reshape(TOKENS, KVHEADS, group, HEAD)
    key_all = key_rows.astype(jnp.float32).reshape(TOKENS, KVHEADS, HEAD)
    value_all = value_rows.astype(jnp.float32).reshape(TOKENS, KVHEADS, HEAD)
    block_width = min(256, TOKENS)
    key_place = jnp.arange(TOKENS)
    score_scale = 1.0 / math.sqrt(HEAD)

    def attend(index):
        first_row = (index * block_width).astype(jnp.int32)
        query_tile_rows = lax.dynamic_slice_in_dim(query_all, first_row, block_width, 0)
        scores = jnp.einsum('tgqd,sgd->tgqs', query_tile_rows, key_all, precision=precise) * score_scale
        query_place = first_row + jnp.arange(block_width)
        visible = (key_place[None, :] <= query_place[:, None])[:, None, None, :]
        scores = jnp.where(visible, scores, -1e+30)
        row_max = lax.optimization_barrier(jnp.max(scores, axis=-1, keepdims=True))
        weights = jnp.where(visible, jnp.exp(scores - row_max), 0.0)
        denominator = lax.optimization_barrier(jnp.sum(weights, axis=-1))
        weights_half = lax.optimization_barrier(weights.astype(jnp.bfloat16))
        numerator = jnp.einsum('tgqs,sgd->tgqd', weights_half.astype(jnp.float32), value_all, precision=precise)
        return (numerator / denominator[..., None]).astype(jnp.bfloat16)
    attn = lax.map(attend, jnp.arange(TOKENS // block_width, dtype=jnp.int32))
    attn = attn.reshape(TOKENS, ASKER_PROBES * HEAD)
    summed = jnp.dot(attn, attn_out_weight, preferred_element_type=jnp.float32)
    summed = summed + jnp.dot(ssm_out, ssm_out_weight, preferred_element_type=jnp.float32)
    return summed
```

```python
import math

import jax
import jax.numpy as jnp
from jax import lax
from jax.experimental import pallas as pl
from jax.experimental.pallas import tpu as pltpu
from jax.sharding import PartitionSpec as P

f32 = jnp.float32
bf16 = jnp.bfloat16
ROWS = 128
HEADS = 6
HDIM = 64
CH = HEADS * HDIM
STATE = 256
GROUP = 16
SUPER = 4
OWN = CH // GROUP
PAD = 32
HEAD = 128
QH = 8
TP = 8
SLICE = 16
D = 2048
LOW = -1e30
SCALE = 1.0 / math.sqrt(HEAD)
HI = lax.Precision.HIGHEST

near = [[GROUP * h + i for i in range(GROUP)] for h in range(SUPER)]
far = [[GROUP * h + i for h in range(SUPER)] for i in range(GROUP)]


def iota(shape, dim):
    return lax.broadcasted_iota(jnp.int32, shape, dim)


def cut(v, parts):
    out = []
    for _ in range(parts):
        hi = v.astype(bf16).astype(f32)
        out.append(hi)
        v = v - hi
    return out


def spread(r, shape, dim, width):
    which = iota(shape, dim) // width
    out = jnp.zeros(shape, f32)
    for h in range(HEADS):
        out = jnp.where(which == h, r[:, h : h + 1], out)
    return out


def nn(a, b):
    return lax.dot_general(a, b, (((1,), (0,)), ((), ())), preferred_element_type=f32)


def nt(a, b):
    return lax.dot_general(a, b, (((1,), (1,)), ((), ())), preferred_element_type=f32)


def tn(a, b):
    return lax.dot_general(a, b, (((0,), (0,)), ((), ())), preferred_element_type=f32)


def states_kernel(x_ref, b_ref, r_ref, out_ref):
    rates = r_ref[...]
    later = (iota((ROWS, ROWS), 1) > iota((ROWS, ROWS), 0)).astype(bf16)
    rx = spread(rates, (ROWS, CH), 1, HDIM)
    after = sum(nn(later, part.astype(bf16)) for part in cut(rx, 3))
    xs = x_ref[...].astype(f32) * jnp.exp(-after)
    hi, lo = cut(xs.T, 2)
    b = b_ref[...]
    state = nn(hi.astype(bf16), b) + nn(lo.astype(bf16), b)
    total = jnp.exp(-jnp.sum(rates, axis=0, keepdims=True))
    shape = (GROUP, 8, STATE)
    which = (iota(shape, 0) * OWN + iota(shape, 2)) // HDIM
    fac = jnp.zeros(shape, f32)
    for h in range(HEADS):
        fac = jnp.where(which == h, total[:, h : h + 1].reshape(1, 1, 1), fac)
    hi, lo = cut(fac, 2)
    sub = iota(shape, 1)
    fac = jnp.where(sub == 0, hi, jnp.where(sub == 1, lo, 0.0))
    fac = jnp.where(iota(shape, 2) < OWN, fac, 0.0)
    out_ref[...] = jnp.concatenate([state.reshape(GROUP, OWN, STATE), fac], axis=1).astype(bf16)


def unpack(block):
    block = block.astype(f32)
    state = block[:OWN]
    row = block[OWN : OWN + 1] + block[OWN + 1 : OWN + 2]
    shape = (OWN, HEAD)
    pick = iota(shape, 0) == iota(shape, 1)
    col = jnp.sum(jnp.where(pick, row[:, :HEAD], 0.0), axis=1, keepdims=True)
    return state, row, col


def decay_rows(row):
    hi, lo = cut(row, 2)
    sub = iota((8, STATE), 0)
    return jnp.where(sub == 0, hi, jnp.where(sub == 1, lo, 0.0))


def total_kernel(ra_ref, k_ref, v_ref, out_ref):
    state = jnp.zeros((OWN, STATE), f32)
    prod = jnp.ones((1, STATE), f32)
    for j in range(GROUP):
        s, row, col = unpack(ra_ref[j])
        state = col * state + s
        prod = prod * row
    packed = jnp.concatenate([state, decay_rows(prod)], axis=0).astype(bf16)
    for h in range(SUPER):
        out_ref[h, 0:SLICE, :] = k_ref[...]
        out_ref[h, SLICE : 2 * SLICE, :] = v_ref[...]
        out_ref[h, 2 * SLICE : 2 * SLICE + PAD, :] = packed


def enter_kernel(ra_ref, rb_ref, out_ref):
    mine = lax.axis_index("seq") // GROUP
    state = jnp.zeros((OWN, STATE), f32)
    for h in range(SUPER - 1):
        s, _, col = unpack(rb_ref[h, 2 * SLICE :, :])
        state = jnp.where(h < mine, col * state + s, state)
    kv = [
        jnp.concatenate([rb_ref[2 * c, 0 : 2 * SLICE, :], rb_ref[2 * c + 1, 0 : 2 * SLICE, :]], axis=0)
        for c in range(2)
    ]
    pad = jnp.zeros((PAD - OWN, STATE), f32)
    for j in range(GROUP):
        out_ref[j, 0:PAD, :] = jnp.concatenate([state, pad], axis=0).astype(bf16)
        out_ref[j, PAD:, :] = kv[j % 2]
        if j < GROUP - 1:
            s, _, col = unpack(ra_ref[j])
            state = col * state + s


def within_kernel(x_ref, g_ref, b_ref, c_ref, r_ref, a_out, b_out):
    rates = r_ref[...]
    keep = iota((ROWS, ROWS), 0) >= iota((ROWS, ROWS), 1)
    upto = keep.astype(bf16)
    gate = g_ref[...].astype(f32)
    sg = gate / (1.0 + jnp.exp(-gate))
    rp = spread(rates, (ROWS, ROWS), 1, 1)
    cs = sum(nn(upto, part.astype(bf16)) for part in cut(rp, 3))
    cst = cs.T
    b_out[...] = jnp.exp(-spread(cs, (ROWS, CH), 1, HDIM)) * sg
    cb = nt(c_ref[...], b_ref[...])
    left = iota((ROWS, 2 * HDIM), 1) < HDIM
    for p in range(HEADS // 2):
        xp = x_ref[:, 2 * HDIM * p : 2 * HDIM * (p + 1)]
        x2 = jnp.concatenate([jnp.where(left, xp, 0), jnp.where(left, 0, xp)], axis=0).astype(bf16)
        ms = []
        for h in (2 * p, 2 * p + 1):
            gap = jnp.where(keep, cst[h : h + 1, :] - cs[:, h : h + 1], LOW)
            ms.append(jnp.exp(gap) * cb)
        hi, lo = cut(jnp.concatenate(ms, axis=1), 2)
        y = nn(hi.astype(bf16), x2) + nn(lo.astype(bf16), x2)
        a_out[:, 2 * HDIM * p : 2 * HDIM * (p + 1)] = y * sg[:, 2 * HDIM * p : 2 * HDIM * (p + 1)]


def attention_kernel(q_ref, own_ref, other_ref, out_ref):
    seq, tp = lax.axis_index("seq"), lax.axis_index("tp")
    core = lax.rem(seq, 2)
    keys = GROUP * SLICE
    n = iota((keys, ROWS), 0)
    place = (n // SLICE) * ROWS + tp * SLICE + n % SLICE
    query = seq * ROWS + iota((keys, ROWS), 1)
    chunks = []
    for ref, half in ((own_ref, core), (other_ref, 1 - core)):
        for hh in range(2):
            first = (2 * half + hh) * (GROUP * ROWS)
            vis = place + first <= query
            chunks.append((ref, hh, jnp.concatenate([vis] * 4, axis=1)))
    for g in range(2):
        lanes = slice(g * HEAD, (g + 1) * HEAD)
        qg = jnp.concatenate(
            [q_ref[:, (4 * g + a) * HEAD : (4 * g + a + 1) * HEAD] for a in range(4)], axis=0
        )
        scores = []
        for ref, hh, vis in chunks:
            kk = ref[:, 32 * hh : 32 * hh + 16, lanes].reshape(keys, HEAD)
            scores.append(jnp.where(vis, nt(kk, qg), LOW))
        peak = scores[0]
        for s in scores[1:]:
            peak = jnp.maximum(peak, s)
        peak = jnp.maximum(jnp.max(peak, axis=0, keepdims=True), 0.1 * LOW)
        total = jnp.zeros((1, 4 * ROWS), f32)
        summed = jnp.zeros((HEAD, 4 * ROWS), f32)
        for s, (ref, hh, vis) in zip(scores, chunks):
            w = jnp.exp2((s - peak) * (SCALE * math.log2(math.e)))
            total = total + jnp.sum(w, axis=0, keepdims=True)
            vv = ref[:, 32 * hh + 16 : 32 * hh + 32, lanes].reshape(keys, HEAD)
            summed = summed + tn(vv, w.astype(bf16))
        parts = cut(peak * SCALE, 3) + cut(total, 3)
        sub = iota((16, 4 * ROWS), 0)
        stats = jnp.zeros((16, 4 * ROWS), f32)
        for k, part in enumerate(parts):
            stats = jnp.where(sub == k, part, stats)
        for a in range(4):
            cols = slice(a * ROWS, (a + 1) * ROWS)
            out_ref[4 * g + a, 0:HEAD, :] = summed[:, cols].astype(bf16)
            out_ref[4 * g + a, HEAD:, :] = stats[:, cols].astype(bf16)


def carry_kernel(s_ref, c_ref, a_ref, b_ref, w_ref, out_ref):
    state = s_ref[:, 0:PAD, :].astype(f32)[:, :OWN, :].reshape(CH, STATE).astype(bf16)
    y = a_ref[...] + b_ref[...] * nt(c_ref[...], state)
    y = y.astype(bf16)
    for k in range(D // 512):
        out_ref[:, 512 * k : 512 * (k + 1)] = nn(y, w_ref[:, 512 * k : 512 * (k + 1)])


def project_kernel(rd_ref, w_ref, p_ref, out_ref):
    peaks, totals = [], []
    for j in range(TP):
        stats = rd_ref[j, HEAD:, :].astype(f32)
        peaks.append(stats[0:1] + stats[1:2] + stats[2:3])
        totals.append(stats[3:4] + stats[4:5] + stats[5:6])
    peak = peaks[0]
    for p in peaks[1:]:
        peak = jnp.maximum(peak, p)
    total = jnp.zeros((1, ROWS), f32)
    summed = jnp.zeros((HEAD, ROWS), f32)
    for j in range(TP):
        scale = jnp.exp(peaks[j] - peak)
        total = total + totals[j] * scale
        summed = summed + rd_ref[j, 0:HEAD, :].astype(f32) * scale
    attn = (summed / total).T.astype(bf16)
    for k in range(D // 512):
        cols = slice(512 * k, 512 * (k + 1))
        out = nn(attn, w_ref[:, cols]) + p_ref[:, cols]
        out_ref[:, :, cols] = out.astype(bf16).reshape(TP, SLICE, 512)


def sum_kernel(re_ref, out_ref):
    out = re_ref[0].astype(f32)
    for j in range(1, TP):
        out = out + re_ref[j].astype(f32)
    out_ref[...] = out


def call(kernel, name, outs, args, flops=0, moved=0, exps=0):
    many = isinstance(outs, list)
    shapes = [jax.ShapeDtypeStruct(s, d) for s, d in (outs if many else [outs])]
    spec = pl.BlockSpec(memory_space=pltpu.VMEM)
    return pl.pallas_call(
        kernel,
        name=name,
        out_shape=shapes if many else shapes[0],
        in_specs=[spec] * len(args),
        out_specs=[spec] * len(shapes) if many else spec,
        compiler_params=pltpu.CompilerParams(vmem_limit_bytes=40 * 2**20),
        cost_estimate=pl.CostEstimate(flops=flops, bytes_accessed=moved, transcendentals=exps),
    )(*args)


def swap(x, axis, groups=None):
    return lax.all_to_all(x, axis, 0, 0, axis_index_groups=groups)


def local(queries, keys, values, x, gate, write, read, rates, w_attn, w_ssm):
    sent = call(states_kernel, "states", ((GROUP, PAD, STATE), bf16), (x, write, rates), 10**8, 10**6)
    ra = swap(sent, "seq", near)
    ya, yb = call(
        within_kernel,
        "within",
        [((ROWS, CH), f32), ((ROWS, CH), f32)],
        (x, gate, write, read, rates),
        10**9,
        10**7,
        2 * 10**5,
    )
    totals = call(total_kernel, "totals", ((SUPER, 64, STATE), bf16), (ra, keys, values), 10**7, 10**6)
    rb = swap(totals, "seq", far)
    enter = call(enter_kernel, "enter", ((GROUP, 96, STATE), bf16), (ra, rb), 10**7, 10**6)
    rc = swap(enter, "seq", near)
    own = rc[:, PAD:, :]
    other = lax.ppermute(own, "seq", [(i, i ^ 1) for i in range(GROUP * SUPER)])
    partial = call(
        attention_kernel,
        "attention",
        ((QH, HEAD + 16, ROWS), bf16),
        (queries, own, other),
        6 * 10**8,
        2 * 10**6,
        10**6,
    )
    rd = swap(partial, "tp")
    ssm = call(carry_kernel, "carry", ((ROWS, D), f32), (rc, read, ya, yb, w_ssm), 10**9, 10**7)
    share = call(project_kernel, "project", ((TP, SLICE, D), bf16), (rd, w_attn, ssm), 10**8, 2 * 10**6)
    re = swap(share, "tp")
    return call(sum_kernel, "total", ((SLICE, D), f32), (re,), 10**6, 10**6)


def solution(mesh):
    placed = (
        P("seq", None),
        P(("seq", "tp"), None),
        P(("seq", "tp"), None),
        P("seq", "tp"),
        P("seq", "tp"),
        P("seq", None),
        P("seq", None),
        P("seq", "tp"),
        P("tp", None),
        P("tp", None),
    )
    return jax.shard_map(
        local, mesh=mesh, in_specs=placed, out_specs=P(("seq", "tp"), None), check_vma=False
    )
```

```python
import math

import jax
import jax.numpy as jnp
from jax import lax
from jax.experimental import pallas as pl
from jax.experimental.pallas import tpu as pltpu
from jax.sharding import PartitionSpec as P

f32 = jnp.float32
bf16 = jnp.bfloat16
ROWS = 128
HEADS = 6
HDIM = 64
CH = HEADS * HDIM
STATE = 256
GROUP = 16
SUPER = 4
OWN = CH // GROUP
PAD = 32
HEAD = 128
TP = 8
SLICE = 16
D = 2048
LOW = -1e30
SCALE = 1.0 / math.sqrt(HEAD)
LOG2 = SCALE * math.log2(math.e)
KV = 64

near = [[GROUP * h + i for i in range(GROUP)] for h in range(SUPER)]
far = [[GROUP * h + i for h in range(SUPER)] for i in range(GROUP)]
row = [[0, 1, 2, 3], [4, 5, 6, 7]]


def iota(shape, dim):
    return lax.broadcasted_iota(jnp.int32, shape, dim)


def cut(v, parts):
    out = []
    for _ in range(parts):
        hi = v.astype(bf16).astype(f32)
        out.append(hi)
        v = v - hi
    return out


def spread(r, shape, dim, width):
    which = iota(shape, dim) // width
    out = jnp.zeros(shape, f32)
    for h in range(HEADS):
        out = jnp.where(which == h, r[:, h : h + 1], out)
    return out


def by_token(r):
    return jnp.concatenate([r, jnp.zeros((ROWS - HEADS, ROWS), f32)], axis=0).T


def nn(a, b):
    return lax.dot_general(a, b, (((1,), (0,)), ((), ())), preferred_element_type=f32)


def nt(a, b):
    return lax.dot_general(a, b, (((1,), (1,)), ((), ())), preferred_element_type=f32)


def tn(a, b):
    return lax.dot_general(a, b, (((0,), (0,)), ((), ())), preferred_element_type=f32)


def states_kernel(
    x_hbm, b_hbm, r_hbm, k_hbm, v_hbm, out_ref, keep_ref, give_ref, x_ref, b_ref, r_ref, k_ref, v_ref, sems
):
    copies = [
        pltpu.make_async_copy(source, target, sems.at[k])
        for k, (source, target) in enumerate(
            [(r_hbm, r_ref), (x_hbm, x_ref), (b_hbm, b_ref), (k_hbm, k_ref), (v_hbm, v_ref)]
        )
    ]
    for copy in copies:
        copy.start()
    for copy in copies:
        copy.wait()
    first = lax.axis_index("tp") < TP // 2
    kv = [
        jnp.concatenate([k_ref[:, HEAD * g : HEAD * (g + 1)], v_ref[:, HEAD * g : HEAD * (g + 1)]], axis=1)
        for g in range(2)
    ]
    keep_ref[...] = jnp.where(first, kv[0], kv[1])
    give_ref[...] = jnp.where(first, kv[1], kv[0])
    rates = by_token(r_ref[...])
    later = (iota((ROWS, ROWS), 1) > iota((ROWS, ROWS), 0)).astype(bf16)
    rx = spread(rates, (ROWS, CH), 1, HDIM)
    after = sum(nn(later, part.astype(bf16)) for part in cut(rx, 3))
    xs = x_ref[...].astype(f32) * jnp.exp(-after)
    hi, lo = cut(xs.T, 2)
    b = b_ref[...]
    state = nn(hi.astype(bf16), b) + nn(lo.astype(bf16), b)
    total = jnp.exp(-jnp.sum(rates, axis=0, keepdims=True))
    shape = (GROUP, 8, STATE)
    which = (iota(shape, 0) * OWN + iota(shape, 2)) // HDIM
    fac = jnp.zeros(shape, f32)
    for h in range(HEADS):
        fac = jnp.where(which == h, total[:, h : h + 1].reshape(1, 1, 1), fac)
    hi, lo = cut(fac, 2)
    sub = iota(shape, 1)
    fac = jnp.where(sub == 0, hi, jnp.where(sub == 1, lo, 0.0))
    fac = jnp.where(iota(shape, 2) < OWN, fac, 0.0)
    out_ref[...] = jnp.concatenate([state.reshape(GROUP, OWN, STATE), fac], axis=1).astype(bf16)


def unpack(block):
    block = block.astype(f32)
    state = block[:OWN]
    row = block[OWN : OWN + 1] + block[OWN + 1 : OWN + 2]
    shape = (OWN, HEAD)
    pick = iota(shape, 0) == iota(shape, 1)
    col = jnp.sum(jnp.where(pick, row[:, :HEAD], 0.0), axis=1, keepdims=True)
    return state, row, col


def decay_rows(row):
    hi, lo = cut(row, 2)
    sub = iota((8, STATE), 0)
    return jnp.where(sub == 0, hi, jnp.where(sub == 1, lo, 0.0))


def total_kernel(ra_ref, keep_ref, got_ref, out_ref):
    state = jnp.zeros((OWN, STATE), f32)
    prod = jnp.ones((1, STATE), f32)
    for j in range(GROUP):
        s, row, col = unpack(ra_ref[j])
        state = col * state + s
        prod = prod * row
    packed = jnp.concatenate([state, decay_rows(prod)], axis=0).astype(bf16)
    for h in range(SUPER):
        out_ref[h, 0:SLICE, :] = keep_ref[...]
        out_ref[h, SLICE : 2 * SLICE, :] = got_ref[...]
        out_ref[h, 2 * SLICE : 2 * SLICE + PAD, :] = packed


def enter_kernel(ra_ref, rb_ref, out_ref):
    mine = lax.axis_index("seq") // GROUP
    state = jnp.zeros((OWN, STATE), f32)
    for h in range(SUPER - 1):
        s, _, col = unpack(rb_ref[h, 2 * SLICE :, :])
        state = jnp.where(h < mine, col * state + s, state)
    kv = [
        jnp.concatenate([rb_ref[2 * c, 0 : 2 * SLICE, :], rb_ref[2 * c + 1, 0 : 2 * SLICE, :]], axis=0).astype(f32)
        for c in range(2)
    ]
    for j in range(GROUP):
        out_ref[j] = jnp.concatenate([kv[j % 2], state], axis=0).astype(bf16)
        if j < GROUP - 1:
            s, _, col = unpack(ra_ref[j])
            state = col * state + s


def within_kernel(x_ref, g_ref, b_ref, c_ref, r_ref, a_out, b_out):
    keep = iota((ROWS, ROWS), 0) >= iota((ROWS, ROWS), 1)
    upto = keep.astype(bf16)
    gate = g_ref[...].astype(f32)
    sg = gate / (1.0 + jnp.exp(-gate))
    cs = sum(nn(upto, part.astype(bf16)) for part in cut(by_token(r_ref[...]), 3))
    cst = cs.T
    b_out[...] = jnp.exp(-spread(cs, (ROWS, CH), 1, HDIM)) * sg
    cb = nt(c_ref[...], b_ref[...])
    left = iota((ROWS, 2 * HDIM), 1) < HDIM
    for p in range(HEADS // 2):
        xp = x_ref[:, 2 * HDIM * p : 2 * HDIM * (p + 1)]
        x2 = jnp.concatenate([jnp.where(left, xp, 0), jnp.where(left, 0, xp)], axis=0).astype(bf16)
        ms = []
        for h in (2 * p, 2 * p + 1):
            gap = jnp.where(keep, cst[h : h + 1, :] - cs[:, h : h + 1], LOW)
            ms.append(jnp.exp(gap) * cb)
        hi, lo = cut(jnp.concatenate(ms, axis=1), 2)
        y = nn(hi.astype(bf16), x2) + nn(lo.astype(bf16), x2)
        a_out[:, 2 * HDIM * p : 2 * HDIM * (p + 1)] = y * sg[:, 2 * HDIM * p : 2 * HDIM * (p + 1)]


def attend(q_ref, kv_ref, half, before):
    seq, tp = lax.axis_index("seq"), lax.axis_index("tp")
    keys = GROUP * 2 * SLICE
    n = iota((keys, ROWS), 0)
    in_pair = n % (2 * SLICE)
    slot = jnp.where(in_pair < SLICE, tp, lax.rem(tp + TP // 2, TP))
    place = (n // (2 * SLICE)) * ROWS + slot * SLICE + n % SLICE
    query = seq * ROWS + iota((keys, ROWS), 1)
    first = tp < TP // 2
    qg = jnp.concatenate(
        [
            jnp.where(first, q_ref[:, a * HEAD : (a + 1) * HEAD], q_ref[:, (4 + a) * HEAD : (5 + a) * HEAD])
            for a in range(4)
        ],
        axis=0,
    )
    scores = []
    for hh in range(2):
        vis = place + (2 * half + hh) * (GROUP * ROWS) <= query
        kk = kv_ref[:, 32 * hh : 32 * hh + 32, 0:HEAD].reshape(keys, HEAD)
        scores.append(jnp.where(jnp.concatenate([vis] * 4, axis=1), nt(kk, qg), LOW))
    peak = jnp.max(jnp.maximum(scores[0], scores[1]), axis=0, keepdims=True)
    peak = jnp.maximum(peak, 0.1 * LOW)
    if before is None:
        total = jnp.zeros((1, 4 * ROWS), f32)
        summed = jnp.zeros((HEAD, 4 * ROWS), f32)
    else:
        old, total, summed = before
        peak = jnp.maximum(peak, old)
        shrink = jnp.exp2((old - peak) * LOG2)
        total, summed = total * shrink, summed * shrink
    for hh in range(2):
        w = jnp.exp2((scores[hh] - peak) * LOG2)
        total = total + jnp.sum(w, axis=0, keepdims=True)
        vv = kv_ref[:, 32 * hh : 32 * hh + 32, HEAD:].reshape(keys, HEAD)
        summed = summed + tn(vv, w.astype(bf16))
    return peak, total, summed


def first_kernel(q_ref, kv_ref, sum_out, stat_out):
    peak, total, summed = attend(q_ref, kv_ref, lax.rem(lax.axis_index("seq"), 2), None)
    sum_out[...] = summed
    stat_out[...] = jnp.where(iota((8, 4 * ROWS), 0) == 0, peak, total)


def second_kernel(q_ref, kv_ref, sum_ref, stat_ref, out_ref):
    before = (stat_ref[0:1, :], stat_ref[1:2, :], sum_ref[...])
    peak, total, summed = attend(q_ref, kv_ref, 1 - lax.rem(lax.axis_index("seq"), 2), before)
    sub = iota((16, 4 * ROWS), 0)
    stats = jnp.zeros((16, 4 * ROWS), f32)
    for k, part in enumerate(cut(peak * SCALE, 3) + cut(total, 3)):
        stats = jnp.where(sub == k, part, stats)
    for a in range(4):
        cols = slice(a * ROWS, (a + 1) * ROWS)
        out_ref[a, 0:HEAD, :] = summed[:, cols].astype(bf16)
        out_ref[a, HEAD:, :] = stats[:, cols].astype(bf16)


def carry_kernel(s_ref, c_ref, a_ref, b_ref, w_ref, after_ref, out_ref):
    state = s_ref[...].astype(f32)[:, KV:, :].reshape(CH, STATE).astype(bf16)
    y = a_ref[...] + b_ref[...] * nt(c_ref[...], state)
    y = y.astype(bf16)
    for k in range(D // 512):
        out_ref[:, 512 * k : 512 * (k + 1)] = nn(y, w_ref[:, 512 * k : 512 * (k + 1)])


def project_kernel(rd_ref, w_ref, p_ref, out_ref):
    peaks, totals = [], []
    for j in range(TP // 2):
        stats = rd_ref[j, HEAD:, :].astype(f32)
        peaks.append(stats[0:1] + stats[1:2] + stats[2:3])
        totals.append(stats[3:4] + stats[4:5] + stats[5:6])
    peak = peaks[0]
    for p in peaks[1:]:
        peak = jnp.maximum(peak, p)
    total = jnp.zeros((1, ROWS), f32)
    summed = jnp.zeros((HEAD, ROWS), f32)
    for j in range(TP // 2):
        scale = jnp.exp(peaks[j] - peak)
        total = total + totals[j] * scale
        summed = summed + rd_ref[j, 0:HEAD, :].astype(f32) * scale
    attn = (summed / total).T.astype(bf16)
    for k in range(D // 512):
        cols = slice(512 * k, 512 * (k + 1))
        out = nn(attn, w_ref[:, cols]) + p_ref[:, cols]
        out_ref[:, :, cols] = out.astype(bf16).reshape(TP, SLICE, 512)


def sum_kernel(re_ref, out_ref):
    out = re_ref[0].astype(f32)
    for j in range(1, TP):
        out = out + re_ref[j].astype(f32)
    out_ref[...] = out


def call(kernel, name, outs, args, flops=0, moved=0, exps=0, left=(), scratch=(), vmem=40):
    many = isinstance(outs, list)
    shapes = [jax.ShapeDtypeStruct(s, d) for s, d in (outs if many else [outs])]
    spec = pl.BlockSpec(memory_space=pltpu.VMEM)
    return pl.pallas_call(
        kernel,
        name=name,
        out_shape=shapes if many else shapes[0],
        in_specs=[pl.BlockSpec(memory_space=pl.ANY) if k in left else spec for k in range(len(args))],
        out_specs=[spec] * len(shapes) if many else spec,
        scratch_shapes=list(scratch),
        compiler_params=pltpu.CompilerParams(vmem_limit_bytes=vmem * 2**20),
        cost_estimate=pl.CostEstimate(flops=flops, bytes_accessed=moved, transcendentals=exps),
    )(*args)


def swap(x, axis, groups=None):
    return lax.all_to_all(x, axis, 0, 0, axis_index_groups=groups)


def local(queries, keys, values, x, gate, write, read, rates, w_attn, w_ssm):
    rates = rates.T
    sent, keep, give = call(
        states_kernel,
        "states",
        [((GROUP, PAD, STATE), bf16), ((SLICE, 2 * HEAD), bf16), ((SLICE, 2 * HEAD), bf16)],
        (x, write, rates, keys, values),
        10**8,
        10**6,
        left=range(5),
        vmem=60,
        scratch=[
            pltpu.VMEM((ROWS, CH), bf16),
            pltpu.VMEM((ROWS, STATE), bf16),
            pltpu.VMEM((HEADS, ROWS), f32),
            pltpu.VMEM((SLICE, 2 * HEAD), bf16),
            pltpu.VMEM((SLICE, 2 * HEAD), bf16),
            pltpu.SemaphoreType.DMA((5,)),
        ],
    )
    ra = swap(sent, "seq", near)
    got = lax.ppermute(give, "tp", [(i, i ^ 4) for i in range(TP)])
    ya, yb = call(
        within_kernel,
        "within",
        [((ROWS, CH), f32), ((ROWS, CH), f32)],
        (x, gate, write, read, rates),
        10**9,
        10**7,
        2 * 10**5,
    )
    totals = call(total_kernel, "totals", ((SUPER, 64, STATE), bf16), (ra, keep, got), 10**7, 10**6)
    rb = swap(totals, "seq", far)
    enter = call(enter_kernel, "enter", ((GROUP, KV + OWN, STATE), bf16), (ra, rb), 10**7, 10**6)
    rc = swap(enter, "seq", near)
    own = rc[:, :KV, :]
    other = lax.ppermute(own, "seq", [(i, i ^ 1) for i in range(GROUP * SUPER)])
    summed, stats = call(
        first_kernel,
        "attend_own",
        [((HEAD, 4 * ROWS), f32), ((8, 4 * ROWS), f32)],
        (queries, own),
        3 * 10**8,
        2 * 10**6,
        5 * 10**5,
    )
    partial = call(
        second_kernel,
        "attend_other",
        ((TP // 2, HEAD + 16, ROWS), bf16),
        (queries, other, summed, stats),
        3 * 10**8,
        2 * 10**6,
        5 * 10**5,
    )
    rd = swap(partial, "tp", row)
    ssm = call(
        carry_kernel, "carry", ((ROWS, D), f32), (rc, read, ya, yb, w_ssm, partial), 10**9, 10**7, left=(5,)
    )
    share = call(project_kernel, "project", ((TP, SLICE, D), bf16), (rd, w_attn, ssm), 10**8, 2 * 10**6)
    re = swap(share, "tp")
    return call(sum_kernel, "total", ((SLICE, D), f32), (re,), 10**6, 10**6)


def solution(mesh):
    placed = (
        P("seq", None),
        P(("seq", "tp"), None),
        P(("seq", "tp"), None),
        P("seq", "tp"),
        P("seq", "tp"),
        P("seq", None),
        P("seq", None),
        P("seq", "tp"),
        P("tp", None),
        P("tp", None),
    )
    return jax.shard_map(
        local, mesh=mesh, in_specs=placed, out_specs=P(("seq", "tp"), None), check_vma=False
    )
```

```python
import math

import jax
import jax.numpy as jnp
from jax import lax
from jax.experimental import pallas as pl
from jax.experimental.pallas import tpu as pltpu
from jax.sharding import PartitionSpec as P

f32 = jnp.float32
bf16 = jnp.bfloat16
ROWS = 128
HEADS = 6
HDIM = 64
CH = HEADS * HDIM
STATE = 256
GROUP = 16
SUPER = 4
OWN = CH // GROUP
PAD = 32
HEAD = 128
QUERY = 1024
TP = 8
SLICE = 16
D = 2048
LOW = -1e30
SCALE = 1.0 / math.sqrt(HEAD)
LOG2 = SCALE * math.log2(math.e)
KV = 32

near = [[GROUP * h + i for i in range(GROUP)] for h in range(SUPER)]
far = [[GROUP * h + i for h in range(SUPER)] for i in range(GROUP)]
heads = [
    [(4 * z + 2 * y_lo + core) * TP + 4 * y_hi + x for y_lo in range(2) for x in range(4)]
    for z in range(GROUP * SUPER // 4)
    for core in range(2)
    for y_hi in range(2)
]


def iota(shape, dim):
    return lax.broadcasted_iota(jnp.int32, shape, dim)


def cut(v, parts):
    out = []
    for _ in range(parts):
        hi = v.astype(bf16).astype(f32)
        out.append(hi)
        v = v - hi
    return out


def spread(r, shape, dim, width):
    which = iota(shape, dim) // width
    out = jnp.zeros(shape, f32)
    for h in range(HEADS):
        out = jnp.where(which == h, r[:, h : h + 1], out)
    return out


def by_token(r):
    return jnp.concatenate([r, jnp.zeros((ROWS - HEADS, ROWS), f32)], axis=0).T


def nn(a, b):
    return lax.dot_general(a, b, (((1,), (0,)), ((), ())), preferred_element_type=f32)


def nt(a, b):
    return lax.dot_general(a, b, (((1,), (1,)), ((), ())), preferred_element_type=f32)


def tn(a, b):
    return lax.dot_general(a, b, (((0,), (0,)), ((), ())), preferred_element_type=f32)


def states_kernel(
    x_hbm, b_hbm, r_hbm, k_hbm, v_hbm, out_ref, keep_ref, give_ref, x_ref, b_ref, r_ref, k_ref, v_ref, sems
):
    copies = [
        pltpu.make_async_copy(source, target, sems.at[k])
        for k, (source, target) in enumerate(
            [(r_hbm, r_ref), (x_hbm, x_ref), (b_hbm, b_ref), (k_hbm, k_ref), (v_hbm, v_ref)]
        )
    ]
    for copy in copies:
        copy.start()
    for copy in copies:
        copy.wait()
    first = lax.axis_index("tp") < TP // 2
    kv = [
        jnp.concatenate([k_ref[:, HEAD * g : HEAD * (g + 1)], v_ref[:, HEAD * g : HEAD * (g + 1)]], axis=1)
        for g in range(2)
    ]
    keep_ref[...] = jnp.where(first, kv[0], kv[1])
    give_ref[...] = jnp.where(first, kv[1], kv[0])
    rates = by_token(r_ref[...])
    later = (iota((ROWS, ROWS), 1) > iota((ROWS, ROWS), 0)).astype(bf16)
    rx = spread(rates, (ROWS, CH), 1, HDIM)
    after = sum(nn(later, part.astype(bf16)) for part in cut(rx, 3))
    xs = x_ref[...].astype(f32) * jnp.exp(-after)
    hi, lo = cut(xs.T, 2)
    b = b_ref[...]
    state = nn(hi.astype(bf16), b) + nn(lo.astype(bf16), b)
    total = jnp.exp(-jnp.sum(rates, axis=0, keepdims=True))
    shape = (GROUP, 8, STATE)
    which = (iota(shape, 0) * OWN + iota(shape, 2)) // HDIM
    fac = jnp.zeros(shape, f32)
    for h in range(HEADS):
        fac = jnp.where(which == h, total[:, h : h + 1].reshape(1, 1, 1), fac)
    hi, lo = cut(fac, 2)
    sub = iota(shape, 1)
    fac = jnp.where(sub == 0, hi, jnp.where(sub == 1, lo, 0.0))
    fac = jnp.where(iota(shape, 2) < OWN, fac, 0.0)
    out_ref[...] = jnp.concatenate([state.reshape(GROUP, OWN, STATE), fac], axis=1).astype(bf16)


def unpack(block):
    block = block.astype(f32)
    state = block[:OWN]
    row = block[OWN : OWN + 1] + block[OWN + 1 : OWN + 2]
    shape = (OWN, HEAD)
    pick = iota(shape, 0) == iota(shape, 1)
    col = jnp.sum(jnp.where(pick, row[:, :HEAD], 0.0), axis=1, keepdims=True)
    return state, row, col


def decay_rows(row):
    hi, lo = cut(row, 2)
    sub = iota((8, STATE), 0)
    return jnp.where(sub == 0, hi, jnp.where(sub == 1, lo, 0.0))


def total_kernel(ra_ref, keep_ref, got_ref, out_ref):
    state = jnp.zeros((OWN, STATE), f32)
    prod = jnp.ones((1, STATE), f32)
    for j in range(GROUP):
        s, row, col = unpack(ra_ref[j])
        state = col * state + s
        prod = prod * row
    packed = jnp.concatenate([state, decay_rows(prod)], axis=0).astype(bf16)
    for h in range(SUPER):
        out_ref[h, 0:SLICE, :] = keep_ref[...]
        out_ref[h, SLICE : 2 * SLICE, :] = got_ref[...]
        out_ref[h, 2 * SLICE : 2 * SLICE + PAD, :] = packed


def pick_kernel(q_ref, after_ref, out_ref):
    half = QUERY // 2
    out_ref[...] = jnp.where(lax.axis_index("tp") < TP // 2, q_ref[:, :half], q_ref[:, half:])


def enter_kernel(ra_ref, rb_ref, after_ref, out_ref):
    mine = lax.axis_index("seq") // GROUP
    state = jnp.zeros((OWN, STATE), f32)
    for h in range(SUPER - 1):
        s, _, col = unpack(rb_ref[h, 2 * SLICE :, :])
        state = jnp.where(h < mine, col * state + s, state)
    kv = [rb_ref[h, 0:KV, :].astype(f32) for h in range(SUPER)]
    for j in range(GROUP):
        out_ref[j] = jnp.concatenate([kv[j % SUPER], state], axis=0).astype(bf16)
        if j < GROUP - 1:
            s, _, col = unpack(ra_ref[j])
            state = col * state + s


def within_kernel(x_ref, g_ref, b_ref, c_ref, r_ref, a_out, b_out):
    keep = iota((ROWS, ROWS), 0) >= iota((ROWS, ROWS), 1)
    upto = keep.astype(bf16)
    gate = g_ref[...].astype(f32)
    sg = gate / (1.0 + jnp.exp(-gate))
    cs = sum(nn(upto, part.astype(bf16)) for part in cut(by_token(r_ref[...]), 3))
    cst = cs.T
    b_out[...] = jnp.exp(-spread(cs, (ROWS, CH), 1, HDIM)) * sg
    cb = nt(c_ref[...], b_ref[...])
    left = iota((ROWS, 2 * HDIM), 1) < HDIM
    for p in range(HEADS // 2):
        xp = x_ref[:, 2 * HDIM * p : 2 * HDIM * (p + 1)]
        x2 = jnp.concatenate([jnp.where(left, xp, 0), jnp.where(left, 0, xp)], axis=0).astype(bf16)
        ms = []
        for h in (2 * p, 2 * p + 1):
            gap = jnp.where(keep, cst[h : h + 1, :] - cs[:, h : h + 1], LOW)
            ms.append(jnp.exp(gap) * cb)
        hi, lo = cut(jnp.concatenate(ms, axis=1), 2)
        y = nn(hi.astype(bf16), x2) + nn(lo.astype(bf16), x2)
        a_out[:, 2 * HDIM * p : 2 * HDIM * (p + 1)] = y * sg[:, 2 * HDIM * p : 2 * HDIM * (p + 1)]


def attend(q_ref, p_ref, kv_ref, part, before):
    seq, tp = lax.axis_index("seq"), lax.axis_index("tp")
    lower = lax.rem(seq // 2, 2) == 0
    low_seq = jnp.where(lower, seq, seq - 2)
    keys = GROUP * KV
    n = iota((keys, ROWS), 0)
    slot = jnp.where(n % KV < SLICE, tp, lax.rem(tp + TP // 2, TP))
    place = (n // KV) * ROWS + slot * SLICE + n % SLICE + part * (GROUP * ROWS)
    query = low_seq * ROWS + iota((keys, ROWS), 1)
    own, other = q_ref[...], p_ref[...]
    blocks = (jnp.where(lower, own, other), jnp.where(lower, other, own))
    qg = jnp.concatenate([q[:, a * HEAD : (a + 1) * HEAD] for q in blocks for a in range(4)], axis=0)
    vis = [place <= query + c * (2 * ROWS) for c in range(2)]
    scores = nt(kv_ref[:, :, 0:HEAD].reshape(keys, HEAD), qg)
    scores = jnp.where(jnp.concatenate(vis[:1] * 4 + vis[1:] * 4, axis=1), scores, LOW)
    peak = jnp.maximum(jnp.max(scores, axis=0, keepdims=True), 0.1 * LOW)
    if before is not None:
        peak = jnp.maximum(peak, before[0])
    w = jnp.exp2((scores - peak) * LOG2)
    total = jnp.sum(w, axis=0, keepdims=True)
    summed = tn(kv_ref[:, :, HEAD:].reshape(keys, HEAD), w.astype(bf16))
    if before is not None:
        shrink = jnp.exp2((before[0] - peak) * LOG2)
        total, summed = total + before[1] * shrink, summed + before[2] * shrink
    return peak, total, summed


def first_kernel(q_ref, p_ref, kv_ref, sum_out, stat_out):
    peak, total, summed = attend(q_ref, p_ref, kv_ref, lax.rem(lax.axis_index("seq"), SUPER), None)
    sum_out[...] = summed
    stat_out[...] = jnp.where(iota((8, TP * ROWS), 0) == 0, peak, total)


def second_kernel(q_ref, p_ref, kv_ref, sum_ref, stat_ref, out_ref):
    before = (stat_ref[0:1, :], stat_ref[1:2, :], sum_ref[...])
    part = lax.rem(lax.axis_index("seq"), SUPER)
    part = part + 1 - 2 * lax.rem(part, 2)
    peak, total, summed = attend(q_ref, p_ref, kv_ref, part, before)
    sub = iota((16, TP * ROWS), 0)
    stats = jnp.zeros((16, TP * ROWS), f32)
    for k, piece in enumerate(cut(peak * SCALE, 3) + cut(total, 3)):
        stats = jnp.where(sub == k, piece, stats)
    for a in range(TP):
        cols = slice(a * ROWS, (a + 1) * ROWS)
        out_ref[a, 0:HEAD, :] = summed[:, cols].astype(bf16)
        out_ref[a, HEAD:, :] = stats[:, cols].astype(bf16)


def carry_kernel(s_ref, c_ref, a_ref, b_ref, w_ref, after_ref, out_ref):
    state = s_ref[...].astype(f32)[:, KV:, :].reshape(CH, STATE).astype(bf16)
    y = a_ref[...] + b_ref[...] * nt(c_ref[...], state)
    y = y.astype(bf16)
    for k in range(D // 512):
        out_ref[:, 512 * k : 512 * (k + 1)] = nn(y, w_ref[:, 512 * k : 512 * (k + 1)])


def project_kernel(rd_ref, w_ref, p_ref, out_ref):
    peaks, totals = [], []
    for j in range(TP):
        stats = rd_ref[j, HEAD:, :].astype(f32)
        peaks.append(stats[0:1] + stats[1:2] + stats[2:3])
        totals.append(stats[3:4] + stats[4:5] + stats[5:6])
    peak = peaks[0]
    for p in peaks[1:]:
        peak = jnp.maximum(peak, p)
    total = jnp.zeros((1, ROWS), f32)
    summed = jnp.zeros((HEAD, ROWS), f32)
    for j in range(TP):
        scale = jnp.exp(peaks[j] - peak)
        total = total + totals[j] * scale
        summed = summed + rd_ref[j, 0:HEAD, :].astype(f32) * scale
    attn = (summed / total).T.astype(bf16)
    for k in range(D // 512):
        cols = slice(512 * k, 512 * (k + 1))
        out = nn(attn, w_ref[:, cols]) + p_ref[:, cols]
        out_ref[:, :, cols] = out.astype(bf16).reshape(TP, SLICE, 512)


def sum_kernel(re_ref, out_ref):
    out = re_ref[0].astype(f32)
    for j in range(1, TP):
        out = out + re_ref[j].astype(f32)
    out_ref[...] = out


def call(kernel, name, outs, args, flops=0, moved=0, exps=0, left=(), scratch=(), vmem=40):
    many = isinstance(outs, list)
    shapes = [jax.ShapeDtypeStruct(s, d) for s, d in (outs if many else [outs])]
    spec = pl.BlockSpec(memory_space=pltpu.VMEM)
    return pl.pallas_call(
        kernel,
        name=name,
        out_shape=shapes if many else shapes[0],
        in_specs=[pl.BlockSpec(memory_space=pl.ANY) if k in left else spec for k in range(len(args))],
        out_specs=[spec] * len(shapes) if many else spec,
        scratch_shapes=list(scratch),
        compiler_params=pltpu.CompilerParams(vmem_limit_bytes=vmem * 2**20),
        cost_estimate=pl.CostEstimate(flops=flops, bytes_accessed=moved, transcendentals=exps),
    )(*args)


def swap(x, axis, groups=None):
    return lax.all_to_all(x, axis, 0, 0, axis_index_groups=groups)


def local(queries, keys, values, x, gate, write, read, rates, w_attn, w_ssm):
    rates = rates.T
    sent, keep, give = call(
        states_kernel,
        "states",
        [((GROUP, PAD, STATE), bf16), ((SLICE, 2 * HEAD), bf16), ((SLICE, 2 * HEAD), bf16)],
        (x, write, rates, keys, values),
        10**8,
        10**6,
        left=range(5),
        vmem=60,
        scratch=[
            pltpu.VMEM((ROWS, CH), bf16),
            pltpu.VMEM((ROWS, STATE), bf16),
            pltpu.VMEM((HEADS, ROWS), f32),
            pltpu.VMEM((SLICE, 2 * HEAD), bf16),
            pltpu.VMEM((SLICE, 2 * HEAD), bf16),
            pltpu.SemaphoreType.DMA((5,)),
        ],
    )
    ra = swap(sent, "seq", near)
    got = lax.ppermute(give, "tp", [(i, i ^ 4) for i in range(TP)])
    ya, yb = call(
        within_kernel,
        "within",
        [((ROWS, CH), f32), ((ROWS, CH), f32)],
        (x, gate, write, read, rates),
        10**9,
        10**7,
        2 * 10**5,
    )
    totals = call(total_kernel, "totals", ((SUPER, 64, STATE), bf16), (ra, keep, got), 10**7, 10**6)
    q_own = call(pick_kernel, "pick", ((ROWS, QUERY // 2), bf16), (queries, totals), 10**7, 10**6, left=(1,))
    q_other = lax.ppermute(q_own, "seq", [(i, i ^ 2) for i in range(GROUP * SUPER)])
    rb = swap(totals, "seq", far)
    enter = call(
        enter_kernel, "enter", ((GROUP, KV + OWN, STATE), bf16), (ra, rb, q_other), 10**7, 10**6, left=(2,)
    )
    rc = swap(enter, "seq", near)
    own = rc[:, :KV, :]
    other = lax.ppermute(own, "seq", [(i, i ^ 1) for i in range(GROUP * SUPER)])
    summed, stats = call(
        first_kernel,
        "attend_own",
        [((HEAD, TP * ROWS), f32), ((8, TP * ROWS), f32)],
        (q_own, q_other, own),
        3 * 10**8,
        2 * 10**6,
        5 * 10**5,
    )
    partial = call(
        second_kernel,
        "attend_other",
        ((TP, HEAD + 16, ROWS), bf16),
        (q_own, q_other, other, summed, stats),
        3 * 10**8,
        2 * 10**6,
        5 * 10**5,
    )
    rd = swap(partial, ("seq", "tp"), heads)
    ssm = call(
        carry_kernel, "carry", ((ROWS, D), f32), (rc, read, ya, yb, w_ssm, partial), 10**9, 10**7, left=(5,)
    )
    share = call(project_kernel, "project", ((TP, SLICE, D), bf16), (rd, w_attn, ssm), 10**8, 2 * 10**6)
    re = swap(share, "tp")
    return call(sum_kernel, "total", ((SLICE, D), f32), (re,), 10**6, 10**6)


def solution(mesh):
    placed = (
        P("seq", None),
        P(("seq", "tp"), None),
        P(("seq", "tp"), None),
        P("seq", "tp"),
        P("seq", "tp"),
        P("seq", None),
        P("seq", None),
        P("seq", "tp"),
        P("tp", None),
        P("tp", None),
    )
    return jax.shard_map(
        local, mesh=mesh, in_specs=placed, out_specs=P(("seq", "tp"), None), check_vma=False
    )
```

```python
import math

import jax
import jax.numpy as jnp
from jax import lax
from jax.experimental import pallas as pl
from jax.experimental.pallas import tpu as pltpu
from jax.sharding import PartitionSpec as P

f32 = jnp.float32
bf16 = jnp.bfloat16
ROWS = 128
HEADS = 6
HDIM = 64
CH = HEADS * HDIM
STATE = 256
GROUP = 16
SUPER = 4
OWN = CH // GROUP
PAD = 32
HEAD = 128
QUERY = 1024
TP = 8
SLICE = 16
D = 2048
LOW = -1e30
SCALE = 1.0 / math.sqrt(HEAD)
LOG2 = SCALE * math.log2(math.e)
KV = 32

near = [[GROUP * h + i for i in range(GROUP)] for h in range(SUPER)]
far = [[GROUP * h + i for h in range(SUPER)] for i in range(GROUP)]
heads = [
    [(4 * z + 2 * y_lo + core) * TP + 4 * y_hi + x for y_lo in range(2) for x in range(4)]
    for z in range(GROUP * SUPER // 4)
    for core in range(2)
    for y_hi in range(2)
]


def iota(shape, dim):
    return lax.broadcasted_iota(jnp.int32, shape, dim)


def cut(v, parts):
    out = []
    for _ in range(parts):
        hi = v.astype(bf16).astype(f32)
        out.append(hi)
        v = v - hi
    return out


def spread(r, shape, dim, width):
    which = iota(shape, dim) // width
    out = jnp.zeros(shape, f32)
    for h in range(HEADS):
        out = jnp.where(which == h, r[:, h : h + 1], out)
    return out


def by_token(r):
    return jnp.concatenate([r, jnp.zeros((ROWS - HEADS, ROWS), f32)], axis=0).T


def nn(a, b):
    return lax.dot_general(a, b, (((1,), (0,)), ((), ())), preferred_element_type=f32)


def nt(a, b):
    return lax.dot_general(a, b, (((1,), (1,)), ((), ())), preferred_element_type=f32)


def tn(a, b):
    return lax.dot_general(a, b, (((0,), (0,)), ((), ())), preferred_element_type=f32)


def states_kernel(
    x_hbm, b_hbm, r_hbm, k_hbm, v_hbm, out_ref, give_ref, x_ref, b_ref, r_ref, k_ref, v_ref, sems
):
    copies = [
        pltpu.make_async_copy(source, target, sems.at[k])
        for k, (source, target) in enumerate(
            [(r_hbm, r_ref), (x_hbm, x_ref), (b_hbm, b_ref), (k_hbm, k_ref), (v_hbm, v_ref)]
        )
    ]
    for copy in copies:
        copy.start()
    copies[0].wait()
    rates = by_token(r_ref[...])
    later = (iota((ROWS, ROWS), 1) > iota((ROWS, ROWS), 0)).astype(bf16)
    after = sum(nn(later, part.astype(bf16)) for part in cut(rates, 3))
    left = jnp.exp(-spread(after, (ROWS, CH), 1, HDIM))
    copies[1].wait()
    xs = x_ref[...].astype(f32) * left
    hi, lo = cut(xs.T, 2)
    copies[2].wait()
    b = b_ref[...]
    state = nn(hi.astype(bf16), b) + nn(lo.astype(bf16), b)
    total = jnp.exp(-jnp.sum(rates, axis=0, keepdims=True))
    shape = (GROUP, 8, STATE)
    which = (iota(shape, 0) * OWN + iota(shape, 2)) // HDIM
    fac = jnp.zeros(shape, f32)
    for h in range(HEADS):
        fac = jnp.where(which == h, total[:, h : h + 1].reshape(1, 1, 1), fac)
    hi, lo = cut(fac, 2)
    sub = iota(shape, 1)
    fac = jnp.where(sub == 0, hi, jnp.where(sub == 1, lo, 0.0))
    fac = jnp.where(iota(shape, 2) < OWN, fac, 0.0)
    out_ref[...] = jnp.concatenate([state.reshape(GROUP, OWN, STATE), fac], axis=1).astype(bf16)
    copies[3].wait()
    copies[4].wait()
    first = lax.axis_index("tp") < TP // 2
    kv = [
        jnp.concatenate([k_ref[:, HEAD * g : HEAD * (g + 1)], v_ref[:, HEAD * g : HEAD * (g + 1)]], axis=1)
        for g in range(2)
    ]
    give_ref[...] = jnp.where(first, kv[1], kv[0])


def unpack(block):
    block = block.astype(f32)
    state = block[:OWN]
    row = block[OWN : OWN + 1] + block[OWN + 1 : OWN + 2]
    shape = (OWN, HEAD)
    pick = iota(shape, 0) == iota(shape, 1)
    col = jnp.sum(jnp.where(pick, row[:, :HEAD], 0.0), axis=1, keepdims=True)
    return state, row, col


def decay_rows(row):
    hi, lo = cut(row, 2)
    sub = iota((8, STATE), 0)
    return jnp.where(sub == 0, hi, jnp.where(sub == 1, lo, 0.0))


def keep_kernel(k_ref, v_ref, out_ref):
    first = lax.axis_index("tp") < TP // 2
    for c, ref in enumerate((k_ref, v_ref)):
        out_ref[:, HEAD * c : HEAD * (c + 1)] = jnp.where(first, ref[:, :HEAD], ref[:, HEAD:])


def total_kernel(ra_ref, keep_ref, got_ref, out_ref):
    state = jnp.zeros((OWN, STATE), f32)
    prod = jnp.ones((1, STATE), f32)
    for j in range(GROUP):
        s, row, col = unpack(ra_ref[j])
        state = col * state + s
        prod = prod * row
    packed = jnp.concatenate([state, decay_rows(prod)], axis=0).astype(bf16)
    for h in range(SUPER):
        out_ref[h, 0:SLICE, :] = keep_ref[...]
        out_ref[h, SLICE : 2 * SLICE, :] = got_ref[...]
        out_ref[h, 2 * SLICE : 2 * SLICE + PAD, :] = packed


def pick_kernel(q_ref, after_ref, out_ref):
    half = QUERY // 2
    out_ref[...] = jnp.where(lax.axis_index("tp") < TP // 2, q_ref[:, :half], q_ref[:, half:])


def enter_kernel(ra_ref, rb_ref, after_ref, out_ref):
    mine = lax.axis_index("seq") // GROUP
    state = jnp.zeros((OWN, STATE), f32)
    for h in range(SUPER - 1):
        s, _, col = unpack(rb_ref[h, 2 * SLICE :, :])
        state = jnp.where(h < mine, col * state + s, state)
    kv = [rb_ref[h, 0:KV, :].astype(f32) for h in range(SUPER)]
    for j in range(GROUP):
        out_ref[j] = jnp.concatenate([kv[j % SUPER], state], axis=0).astype(bf16)
        if j < GROUP - 1:
            s, _, col = unpack(ra_ref[j])
            state = col * state + s


def within_kernel(x_ref, g_ref, b_ref, c_ref, r_ref, a_out, b_out):
    keep = iota((ROWS, ROWS), 0) >= iota((ROWS, ROWS), 1)
    upto = keep.astype(bf16)
    gate = g_ref[...].astype(f32)
    sg = gate / (1.0 + jnp.exp(-gate))
    cs = sum(nn(upto, part.astype(bf16)) for part in cut(by_token(r_ref[...]), 3))
    cst = cs.T
    b_out[...] = jnp.exp(-spread(cs, (ROWS, CH), 1, HDIM)) * sg
    cb = nt(c_ref[...], b_ref[...])
    left = iota((ROWS, 2 * HDIM), 1) < HDIM
    for p in range(HEADS // 2):
        xp = x_ref[:, 2 * HDIM * p : 2 * HDIM * (p + 1)]
        x2 = jnp.concatenate([jnp.where(left, xp, 0), jnp.where(left, 0, xp)], axis=0).astype(bf16)
        ms = []
        for h in (2 * p, 2 * p + 1):
            gap = jnp.where(keep, cst[h : h + 1, :] - cs[:, h : h + 1], LOW)
            ms.append(jnp.exp(gap) * cb)
        hi, lo = cut(jnp.concatenate(ms, axis=1), 2)
        y = nn(hi.astype(bf16), x2) + nn(lo.astype(bf16), x2)
        a_out[:, 2 * HDIM * p : 2 * HDIM * (p + 1)] = y * sg[:, 2 * HDIM * p : 2 * HDIM * (p + 1)]


def attend(q_ref, p_ref, kv_ref, part, before):
    seq, tp = lax.axis_index("seq"), lax.axis_index("tp")
    lower = lax.rem(seq // 2, 2) == 0
    low_seq = jnp.where(lower, seq, seq - 2)
    keys = GROUP * KV
    n = iota((keys, ROWS), 0)
    slot = jnp.where(n % KV < SLICE, tp, lax.rem(tp + TP // 2, TP))
    place = (n // KV) * ROWS + slot * SLICE + n % SLICE + part * (GROUP * ROWS)
    query = low_seq * ROWS + iota((keys, ROWS), 1)
    own, other = q_ref[...], p_ref[...]
    blocks = (jnp.where(lower, own, other), jnp.where(lower, other, own))
    qg = jnp.concatenate([q[:, a * HEAD : (a + 1) * HEAD] for q in blocks for a in range(4)], axis=0)
    vis = [place <= query + c * (2 * ROWS) for c in range(2)]
    scores = nt(kv_ref[:, :, 0:HEAD].reshape(keys, HEAD), qg)
    scores = jnp.where(jnp.concatenate(vis[:1] * 4 + vis[1:] * 4, axis=1), scores, LOW)
    peak = jnp.maximum(jnp.max(scores, axis=0, keepdims=True), 0.1 * LOW)
    if before is not None:
        peak = jnp.maximum(peak, before[0])
    w = jnp.exp2((scores - peak) * LOG2)
    total = jnp.sum(w, axis=0, keepdims=True)
    summed = tn(kv_ref[:, :, HEAD:].reshape(keys, HEAD), w.astype(bf16))
    if before is not None:
        shrink = jnp.exp2((before[0] - peak) * LOG2)
        total, summed = total + before[1] * shrink, summed + before[2] * shrink
    return peak, total, summed


def first_kernel(q_ref, p_ref, kv_ref, sum_out, stat_out):
    peak, total, summed = attend(q_ref, p_ref, kv_ref, lax.rem(lax.axis_index("seq"), SUPER), None)
    sum_out[...] = summed
    stat_out[...] = jnp.where(iota((8, TP * ROWS), 0) == 0, peak, total)


def second_kernel(q_ref, p_ref, kv_ref, sum_ref, stat_ref, out_ref):
    before = (stat_ref[0:1, :], stat_ref[1:2, :], sum_ref[...])
    part = lax.rem(lax.axis_index("seq"), SUPER)
    part = part + 1 - 2 * lax.rem(part, 2)
    peak, total, summed = attend(q_ref, p_ref, kv_ref, part, before)
    sub = iota((16, TP * ROWS), 0)
    stats = jnp.zeros((16, TP * ROWS), f32)
    for k, piece in enumerate(cut(peak * SCALE, 3) + cut(total, 3)):
        stats = jnp.where(sub == k, piece, stats)
    for a in range(TP):
        cols = slice(a * ROWS, (a + 1) * ROWS)
        out_ref[a, 0:HEAD, :] = summed[:, cols].astype(bf16)
        out_ref[a, HEAD:, :] = stats[:, cols].astype(bf16)


def carry_kernel(s_ref, c_ref, a_ref, b_ref, w_ref, after_ref, out_ref):
    state = s_ref[...].astype(f32)[:, KV:, :].reshape(CH, STATE).astype(bf16)
    y = a_ref[...] + b_ref[...] * nt(c_ref[...], state)
    y = y.astype(bf16)
    for k in range(D // 512):
        out_ref[:, 512 * k : 512 * (k + 1)] = nn(y, w_ref[:, 512 * k : 512 * (k + 1)])


def project_kernel(rd_ref, w_ref, p_ref, out_ref):
    peaks, totals = [], []
    for j in range(TP):
        stats = rd_ref[j, HEAD:, :].astype(f32)
        peaks.append(stats[0:1] + stats[1:2] + stats[2:3])
        totals.append(stats[3:4] + stats[4:5] + stats[5:6])
    peak = peaks[0]
    for p in peaks[1:]:
        peak = jnp.maximum(peak, p)
    total = jnp.zeros((1, ROWS), f32)
    summed = jnp.zeros((HEAD, ROWS), f32)
    for j in range(TP):
        scale = jnp.exp(peaks[j] - peak)
        total = total + totals[j] * scale
        summed = summed + rd_ref[j, 0:HEAD, :].astype(f32) * scale
    attn = (summed / total).T.astype(bf16)
    for k in range(D // 512):
        cols = slice(512 * k, 512 * (k + 1))
        out = nn(attn, w_ref[:, cols]) + p_ref[:, cols]
        out_ref[:, :, cols] = out.astype(bf16).reshape(TP, SLICE, 512)


def sum_kernel(re_ref, out_ref):
    out = re_ref[0].astype(f32)
    for j in range(1, TP):
        out = out + re_ref[j].astype(f32)
    out_ref[...] = out


def call(kernel, name, outs, args, flops=0, moved=0, exps=0, left=(), scratch=(), vmem=40):
    many = isinstance(outs, list)
    shapes = [jax.ShapeDtypeStruct(s, d) for s, d in (outs if many else [outs])]
    spec = pl.BlockSpec(memory_space=pltpu.VMEM)
    return pl.pallas_call(
        kernel,
        name=name,
        out_shape=shapes if many else shapes[0],
        in_specs=[pl.BlockSpec(memory_space=pl.ANY) if k in left else spec for k in range(len(args))],
        out_specs=[spec] * len(shapes) if many else spec,
        scratch_shapes=list(scratch),
        compiler_params=pltpu.CompilerParams(vmem_limit_bytes=vmem * 2**20),
        cost_estimate=pl.CostEstimate(flops=flops, bytes_accessed=moved, transcendentals=exps),
    )(*args)


def swap(x, axis, groups=None):
    return lax.all_to_all(x, axis, 0, 0, axis_index_groups=groups)


def local(queries, keys, values, x, gate, write, read, rates, w_attn, w_ssm):
    rates = rates.T
    sent, give = call(
        states_kernel,
        "states",
        [((GROUP, PAD, STATE), bf16), ((SLICE, 2 * HEAD), bf16)],
        (x, write, rates, keys, values),
        10**8,
        10**6,
        left=range(5),
        vmem=60,
        scratch=[
            pltpu.VMEM((ROWS, CH), bf16),
            pltpu.VMEM((ROWS, STATE), bf16),
            pltpu.VMEM((HEADS, ROWS), f32),
            pltpu.VMEM((SLICE, 2 * HEAD), bf16),
            pltpu.VMEM((SLICE, 2 * HEAD), bf16),
            pltpu.SemaphoreType.DMA((5,)),
        ],
    )
    ra = swap(sent, "seq", near)
    got = lax.ppermute(give, "tp", [(i, i ^ 4) for i in range(TP)])
    keep = call(keep_kernel, "keep", ((SLICE, 2 * HEAD), bf16), (keys, values), 10**7, 10**6)
    ya, yb = call(
        within_kernel,
        "within",
        [((ROWS, CH), f32), ((ROWS, CH), f32)],
        (x, gate, write, read, rates),
        10**9,
        10**7,
        2 * 10**5,
    )
    totals = call(total_kernel, "totals", ((SUPER, 64, STATE), bf16), (ra, keep, got), 10**7, 10**6)
    q_own = call(pick_kernel, "pick", ((ROWS, QUERY // 2), bf16), (queries, totals), 10**7, 10**6, left=(1,))
    q_other = lax.ppermute(q_own, "seq", [(i, i ^ 2) for i in range(GROUP * SUPER)])
    rb = swap(totals, "seq", far)
    enter = call(
        enter_kernel, "enter", ((GROUP, KV + OWN, STATE), bf16), (ra, rb, q_other), 10**7, 10**6, left=(2,)
    )
    rc = swap(enter, "seq", near)
    own = rc[:, :KV, :]
    other = lax.ppermute(own, "seq", [(i, i ^ 1) for i in range(GROUP * SUPER)])
    summed, stats = call(
        first_kernel,
        "attend_own",
        [((HEAD, TP * ROWS), f32), ((8, TP * ROWS), f32)],
        (q_own, q_other, own),
        3 * 10**8,
        2 * 10**6,
        5 * 10**5,
    )
    partial = call(
        second_kernel,
        "attend_other",
        ((TP, HEAD + 16, ROWS), bf16),
        (q_own, q_other, other, summed, stats),
        3 * 10**8,
        2 * 10**6,
        5 * 10**5,
    )
    rd = swap(partial, ("seq", "tp"), heads)
    ssm = call(
        carry_kernel, "carry", ((ROWS, D), f32), (rc, read, ya, yb, w_ssm, partial), 10**9, 10**7, left=(5,)
    )
    share = call(project_kernel, "project", ((TP, SLICE, D), bf16), (rd, w_attn, ssm), 10**8, 2 * 10**6)
    re = swap(share, "tp")
    return call(sum_kernel, "total", ((SLICE, D), f32), (re,), 10**6, 10**6)


def solution(mesh):
    placed = (
        P("seq", None),
        P(("seq", "tp"), None),
        P(("seq", "tp"), None),
        P("seq", "tp"),
        P("seq", "tp"),
        P("seq", None),
        P("seq", None),
        P("seq", "tp"),
        P("tp", None),
        P("tp", None),
    )
    return jax.shard_map(
        local, mesh=mesh, in_specs=placed, out_specs=P(("seq", "tp"), None), check_vma=False
    )
```

```python
import math

import jax
import jax.numpy as jnp
from jax import lax
from jax.experimental import pallas as pl
from jax.experimental.pallas import tpu as pltpu
from jax.sharding import PartitionSpec as P

f32 = jnp.float32
bf16 = jnp.bfloat16
ROWS = 128
HEADS = 6
HDIM = 64
CH = HEADS * HDIM
STATE = 256
GROUP = 16
SUPER = 4
OWN = CH // GROUP
PAD = 32
HEAD = 128
QUERY = 1024
TP = 8
SLICE = 16
D = 2048
LOW = -1e30
SCALE = 1.0 / math.sqrt(HEAD)
LOG2 = SCALE * math.log2(math.e)
GIVE = SLICE + 2 * ROWS
KV = 32

near = [[GROUP * h + i for i in range(GROUP)] for h in range(SUPER)]
far = [[GROUP * h + i for h in range(SUPER)] for i in range(GROUP)]
heads = [
    [(4 * z + 2 * y_lo + core) * TP + 4 * y_hi + x for y_lo in range(2) for x in range(4)]
    for z in range(GROUP * SUPER // 4)
    for core in range(2)
    for y_hi in range(2)
]


def iota(shape, dim):
    return lax.broadcasted_iota(jnp.int32, shape, dim)


def cut(v, parts):
    out = []
    for _ in range(parts):
        hi = v.astype(bf16).astype(f32)
        out.append(hi)
        v = v - hi
    return out


def spread(r, shape, dim, width):
    which = iota(shape, dim) // width
    out = jnp.zeros(shape, f32)
    for h in range(HEADS):
        out = jnp.where(which == h, r[:, h : h + 1], out)
    return out


def by_token(r):
    return jnp.concatenate([r, jnp.zeros((ROWS - HEADS, ROWS), f32)], axis=0).T


def nn(a, b):
    return lax.dot_general(a, b, (((1,), (0,)), ((), ())), preferred_element_type=f32)


def nt(a, b):
    return lax.dot_general(a, b, (((1,), (1,)), ((), ())), preferred_element_type=f32)


def tn(a, b):
    return lax.dot_general(a, b, (((0,), (0,)), ((), ())), preferred_element_type=f32)


def states_kernel(
    x_hbm, b_hbm, r_hbm, k_hbm, v_hbm, q_hbm, out_ref, give_ref, x_ref, b_ref, r_ref, k_ref, v_ref, sems
):
    copies = [
        pltpu.make_async_copy(source, target, sems.at[k])
        for k, (source, target) in enumerate(
            [(r_hbm, r_ref), (x_hbm, x_ref), (b_hbm, b_ref), (k_hbm, k_ref), (v_hbm, v_ref)]
        )
    ]
    first = lax.axis_index("tp") < TP // 2
    for c in range(2):
        lanes = pl.ds(pl.multiple_of(jnp.where(first, QUERY // 2, 0) + 2 * HEAD * c, 2 * HEAD), 2 * HEAD)
        rows = slice(SLICE + ROWS * c, SLICE + ROWS * (c + 1))
        copies.append(pltpu.make_async_copy(q_hbm.at[:, lanes], give_ref.at[rows], sems.at[5 + c]))
    for copy in copies:
        copy.start()
    copies[0].wait()
    rates = by_token(r_ref[...])
    later = (iota((ROWS, ROWS), 1) > iota((ROWS, ROWS), 0)).astype(bf16)
    after = sum(nn(later, part.astype(bf16)) for part in cut(rates, 3))
    left = jnp.exp(-spread(after, (ROWS, CH), 1, HDIM))
    copies[1].wait()
    xs = x_ref[...].astype(f32) * left
    hi, lo = cut(xs.T, 2)
    copies[2].wait()
    b = b_ref[...]
    state = nn(hi.astype(bf16), b) + nn(lo.astype(bf16), b)
    total = jnp.exp(-jnp.sum(rates, axis=0, keepdims=True))
    shape = (GROUP, 8, STATE)
    which = (iota(shape, 0) * OWN + iota(shape, 2)) // HDIM
    fac = jnp.zeros(shape, f32)
    for h in range(HEADS):
        fac = jnp.where(which == h, total[:, h : h + 1].reshape(1, 1, 1), fac)
    hi, lo = cut(fac, 2)
    sub = iota(shape, 1)
    fac = jnp.where(sub == 0, hi, jnp.where(sub == 1, lo, 0.0))
    fac = jnp.where(iota(shape, 2) < OWN, fac, 0.0)
    out_ref[...] = jnp.concatenate([state.reshape(GROUP, OWN, STATE), fac], axis=1).astype(bf16)
    for copy in copies[3:]:
        copy.wait()
    kv = [
        jnp.concatenate([k_ref[:, HEAD * g : HEAD * (g + 1)], v_ref[:, HEAD * g : HEAD * (g + 1)]], axis=1)
        for g in range(2)
    ]
    give_ref[0:SLICE, :] = jnp.where(first, kv[1], kv[0])


def unpack(block):
    block = block.astype(f32)
    state = block[:OWN]
    row = block[OWN : OWN + 1] + block[OWN + 1 : OWN + 2]
    shape = (OWN, HEAD)
    pick = iota(shape, 0) == iota(shape, 1)
    col = jnp.sum(jnp.where(pick, row[:, :HEAD], 0.0), axis=1, keepdims=True)
    return state, row, col


def decay_rows(row):
    hi, lo = cut(row, 2)
    sub = iota((8, STATE), 0)
    return jnp.where(sub == 0, hi, jnp.where(sub == 1, lo, 0.0))


def keep_kernel(k_ref, v_ref, out_ref):
    first = lax.axis_index("tp") < TP // 2
    for c, ref in enumerate((k_ref, v_ref)):
        out_ref[:, HEAD * c : HEAD * (c + 1)] = jnp.where(first, ref[:, :HEAD], ref[:, HEAD:])


def total_kernel(ra_ref, keep_ref, got_ref, out_ref):
    state = jnp.zeros((OWN, STATE), f32)
    prod = jnp.ones((1, STATE), f32)
    for j in range(GROUP):
        s, row, col = unpack(ra_ref[j])
        state = col * state + s
        prod = prod * row
    packed = jnp.concatenate([state, decay_rows(prod)], axis=0).astype(bf16)
    for h in range(SUPER):
        out_ref[h, 0:SLICE, :] = keep_ref[...]
        out_ref[h, SLICE : 2 * SLICE, :] = got_ref[0:SLICE, :]
        out_ref[h, 2 * SLICE : 2 * SLICE + PAD, :] = packed


def enter_kernel(ra_ref, rb_ref, out_ref):
    mine = lax.axis_index("seq") // GROUP
    state = jnp.zeros((OWN, STATE), f32)
    for h in range(SUPER - 1):
        s, _, col = unpack(rb_ref[h, 2 * SLICE :, :])
        state = jnp.where(h < mine, col * state + s, state)
    kv = [rb_ref[h, 0:KV, :].astype(f32) for h in range(SUPER)]
    for j in range(GROUP):
        out_ref[j] = jnp.concatenate([kv[j % SUPER], state], axis=0).astype(bf16)
        if j < GROUP - 1:
            s, _, col = unpack(ra_ref[j])
            state = col * state + s


def within_kernel(x_ref, g_ref, b_ref, c_ref, r_ref, a_out, b_out):
    keep = iota((ROWS, ROWS), 0) >= iota((ROWS, ROWS), 1)
    upto = keep.astype(bf16)
    gate = g_ref[...].astype(f32)
    sg = gate / (1.0 + jnp.exp(-gate))
    cs = sum(nn(upto, part.astype(bf16)) for part in cut(by_token(r_ref[...]), 3))
    cst = cs.T
    b_out[...] = jnp.exp(-spread(cs, (ROWS, CH), 1, HDIM)) * sg
    cb = nt(c_ref[...], b_ref[...])
    left = iota((ROWS, 2 * HDIM), 1) < HDIM
    for p in range(HEADS // 2):
        xp = x_ref[:, 2 * HDIM * p : 2 * HDIM * (p + 1)]
        x2 = jnp.concatenate([jnp.where(left, xp, 0), jnp.where(left, 0, xp)], axis=0).astype(bf16)
        ms = []
        for h in (2 * p, 2 * p + 1):
            gap = jnp.where(keep, cst[h : h + 1, :] - cs[:, h : h + 1], LOW)
            ms.append(jnp.exp(gap) * cb)
        hi, lo = cut(jnp.concatenate(ms, axis=1), 2)
        y = nn(hi.astype(bf16), x2) + nn(lo.astype(bf16), x2)
        a_out[:, 2 * HDIM * p : 2 * HDIM * (p + 1)] = y * sg[:, 2 * HDIM * p : 2 * HDIM * (p + 1)]


def attend(q_ref, p_ref, kv_ref, part, before):
    seq, tp = lax.axis_index("seq"), lax.axis_index("tp")
    lower = lax.rem(seq // 2, 2) == 0
    low_seq = jnp.where(lower, seq, seq - 2)
    keys = GROUP * KV
    n = iota((keys, ROWS), 0)
    mine = n % KV < SLICE
    slot = jnp.where(mine, tp, lax.rem(tp + TP // 2, TP))
    block = jnp.where(mine, n // KV, (n // KV) ^ 2)
    place = block * ROWS + slot * SLICE + n % SLICE + part * (GROUP * ROWS)
    query = low_seq * ROWS + iota((keys, ROWS), 1)
    first = tp < TP // 2
    own, other = [], []
    for a in range(4):
        own.append(jnp.where(first, q_ref[:, a * HEAD : (a + 1) * HEAD], q_ref[:, (4 + a) * HEAD : (5 + a) * HEAD]))
        rows = slice(SLICE + ROWS * (a // 2), SLICE + ROWS * (a // 2 + 1))
        other.append(p_ref[rows, HEAD * (a % 2) : HEAD * (a % 2 + 1)])
    own, other = jnp.concatenate(own, axis=0), jnp.concatenate(other, axis=0)
    qg = jnp.concatenate([jnp.where(lower, own, other), jnp.where(lower, other, own)], axis=0)
    vis = [place <= query + c * (2 * ROWS) for c in range(2)]
    scores = nt(kv_ref[:, :, 0:HEAD].reshape(keys, HEAD), qg)
    scores = jnp.where(jnp.concatenate(vis[:1] * 4 + vis[1:] * 4, axis=1), scores, LOW)
    peak = jnp.maximum(jnp.max(scores, axis=0, keepdims=True), 0.1 * LOW)
    if before is not None:
        peak = jnp.maximum(peak, before[0])
    w = jnp.exp2((scores - peak) * LOG2)
    total = jnp.sum(w, axis=0, keepdims=True)
    summed = tn(kv_ref[:, :, HEAD:].reshape(keys, HEAD), w.astype(bf16))
    if before is not None:
        shrink = jnp.exp2((before[0] - peak) * LOG2)
        total, summed = total + before[1] * shrink, summed + before[2] * shrink
    return peak, total, summed


def first_kernel(q_ref, p_ref, kv_ref, sum_out, stat_out):
    peak, total, summed = attend(q_ref, p_ref, kv_ref, lax.rem(lax.axis_index("seq"), SUPER), None)
    sum_out[...] = summed
    stat_out[...] = jnp.where(iota((8, TP * ROWS), 0) == 0, peak, total)


def second_kernel(q_ref, p_ref, kv_ref, sum_ref, stat_ref, out_ref):
    before = (stat_ref[0:1, :], stat_ref[1:2, :], sum_ref[...])
    part = lax.rem(lax.axis_index("seq"), SUPER)
    part = part + 1 - 2 * lax.rem(part, 2)
    peak, total, summed = attend(q_ref, p_ref, kv_ref, part, before)
    sub = iota((16, TP * ROWS), 0)
    stats = jnp.zeros((16, TP * ROWS), f32)
    for k, piece in enumerate(cut(peak * SCALE, 3) + cut(total, 3)):
        stats = jnp.where(sub == k, piece, stats)
    for a in range(TP):
        cols = slice(a * ROWS, (a + 1) * ROWS)
        out_ref[a, 0:HEAD, :] = summed[:, cols].astype(bf16)
        out_ref[a, HEAD:, :] = stats[:, cols].astype(bf16)


def carry_kernel(s_ref, c_ref, a_ref, b_ref, w_ref, after_ref, out_ref):
    state = s_ref[...].astype(f32)[:, KV:, :].reshape(CH, STATE).astype(bf16)
    y = a_ref[...] + b_ref[...] * nt(c_ref[...], state)
    y = y.astype(bf16)
    for k in range(D // 512):
        out_ref[:, 512 * k : 512 * (k + 1)] = nn(y, w_ref[:, 512 * k : 512 * (k + 1)])


def project_kernel(rd_ref, w_ref, p_ref, out_ref):
    peaks, totals = [], []
    for j in range(TP):
        stats = rd_ref[j, HEAD:, :].astype(f32)
        peaks.append(stats[0:1] + stats[1:2] + stats[2:3])
        totals.append(stats[3:4] + stats[4:5] + stats[5:6])
    peak = peaks[0]
    for p in peaks[1:]:
        peak = jnp.maximum(peak, p)
    total = jnp.zeros((1, ROWS), f32)
    summed = jnp.zeros((HEAD, ROWS), f32)
    for j in range(TP):
        scale = jnp.exp(peaks[j] - peak)
        total = total + totals[j] * scale
        summed = summed + rd_ref[j, 0:HEAD, :].astype(f32) * scale
    attn = (summed / total).T.astype(bf16)
    for k in range(D // 512):
        cols = slice(512 * k, 512 * (k + 1))
        out = nn(attn, w_ref[:, cols]) + p_ref[:, cols]
        out_ref[:, :, cols] = out.astype(bf16).reshape(TP, SLICE, 512)


def sum_kernel(re_ref, out_ref):
    out = re_ref[0].astype(f32)
    for j in range(1, TP):
        out = out + re_ref[j].astype(f32)
    out_ref[...] = out


def call(kernel, name, outs, args, flops=0, moved=0, exps=0, left=(), scratch=(), vmem=40):
    many = isinstance(outs, list)
    shapes = [jax.ShapeDtypeStruct(s, d) for s, d in (outs if many else [outs])]
    spec = pl.BlockSpec(memory_space=pltpu.VMEM)
    return pl.pallas_call(
        kernel,
        name=name,
        out_shape=shapes if many else shapes[0],
        in_specs=[pl.BlockSpec(memory_space=pl.ANY) if k in left else spec for k in range(len(args))],
        out_specs=[spec] * len(shapes) if many else spec,
        scratch_shapes=list(scratch),
        compiler_params=pltpu.CompilerParams(vmem_limit_bytes=vmem * 2**20),
        cost_estimate=pl.CostEstimate(flops=flops, bytes_accessed=moved, transcendentals=exps),
    )(*args)


def swap(x, axis, groups=None):
    return lax.all_to_all(x, axis, 0, 0, axis_index_groups=groups)


def local(queries, keys, values, x, gate, write, read, rates, w_attn, w_ssm):
    rates = rates.T
    sent, give = call(
        states_kernel,
        "states",
        [((GROUP, PAD, STATE), bf16), ((GIVE, 2 * HEAD), bf16)],
        (x, write, rates, keys, values, queries),
        10**8,
        10**6,
        left=range(6),
        vmem=60,
        scratch=[
            pltpu.VMEM((ROWS, CH), bf16),
            pltpu.VMEM((ROWS, STATE), bf16),
            pltpu.VMEM((HEADS, ROWS), f32),
            pltpu.VMEM((SLICE, 2 * HEAD), bf16),
            pltpu.VMEM((SLICE, 2 * HEAD), bf16),
            pltpu.SemaphoreType.DMA((7,)),
        ],
    )
    ra = swap(sent, "seq", near)
    got = lax.ppermute(give, ("seq", "tp"), [(i, i ^ (2 * TP + 4)) for i in range(GROUP * SUPER * TP)])
    keep = call(keep_kernel, "keep", ((SLICE, 2 * HEAD), bf16), (keys, values), 10**7, 10**6)
    ya, yb = call(
        within_kernel,
        "within",
        [((ROWS, CH), f32), ((ROWS, CH), f32)],
        (x, gate, write, read, rates),
        10**9,
        10**7,
        2 * 10**5,
    )
    totals = call(total_kernel, "totals", ((SUPER, 64, STATE), bf16), (ra, keep, got), 10**7, 10**6)
    rb = swap(totals, "seq", far)
    enter = call(enter_kernel, "enter", ((GROUP, KV + OWN, STATE), bf16), (ra, rb), 10**7, 10**6)
    rc = swap(enter, "seq", near)
    own = rc[:, :KV, :]
    other = lax.ppermute(own, "seq", [(i, i ^ 1) for i in range(GROUP * SUPER)])
    summed, stats = call(
        first_kernel,
        "attend_own",
        [((HEAD, TP * ROWS), f32), ((8, TP * ROWS), f32)],
        (queries, got, own),
        3 * 10**8,
        2 * 10**6,
        5 * 10**5,
    )
    partial = call(
        second_kernel,
        "attend_other",
        ((TP, HEAD + 16, ROWS), bf16),
        (queries, got, other, summed, stats),
        3 * 10**8,
        2 * 10**6,
        5 * 10**5,
    )
    rd = swap(partial, ("seq", "tp"), heads)
    ssm = call(
        carry_kernel, "carry", ((ROWS, D), f32), (rc, read, ya, yb, w_ssm, partial), 10**9, 10**7, left=(5,)
    )
    share = call(project_kernel, "project", ((TP, SLICE, D), bf16), (rd, w_attn, ssm), 10**8, 2 * 10**6)
    re = swap(share, "tp")
    return call(sum_kernel, "total", ((SLICE, D), f32), (re,), 10**6, 10**6)


def solution(mesh):
    placed = (
        P("seq", None),
        P(("seq", "tp"), None),
        P(("seq", "tp"), None),
        P("seq", "tp"),
        P("seq", "tp"),
        P("seq", None),
        P("seq", None),
        P("seq", "tp"),
        P("tp", None),
        P("tp", None),
    )
    return jax.shard_map(
        local, mesh=mesh, in_specs=placed, out_specs=P(("seq", "tp"), None), check_vma=False
    )
```
